32 devices in a mesh: dp: 4 (over y, x), expert: 8 (over z, core).
Axes of the slice: x: 2, y: 2, z: 4, core: 2. Of those that a mesh axis runs over, the one named last changes fastest.
Arguments:
- tokens: bfloat16 [4096, 1536], P(('dp', 'expert')), may hold values from -6 to 6
- gate_prob: float32 [4096], P(('dp', 'expert')), may hold values from 0.2 to 1
- expert_index: int32 [4096], P(('dp', 'expert')), may hold values from 0 to 15, as said below
- slot_index: int32 [4096], P(('dp', 'expert')), may hold values from 0 to 127, as said below
- dropped: int32 [4096], P(('dp', 'expert')), may hold values from 0 to 1
- cotangent: bfloat16 [4096, 1536], P(('dp', 'expert')), may hold values from -6 to 6
- expert_in: bfloat16 [16, 1536, 6144], P('expert', None, 'dp'), may hold values from -0.15625 to 0.15625
- expert_out: bfloat16 [16, 6144, 1536], P('expert', 'dp'), may hold values from -0.078125 to 0.078125
- residual_in: bfloat16 [1536, 3072], P(None, 'dp'), may hold values from -0.15625 to 0.15625
- residual_out: bfloat16 [3072, 1536], P('dp'), may hold values from -0.109375 to 0.109375
Outputs:
- output: bfloat16 [4096, 1536], P(('dp', 'expert'))
- grad_tokens: bfloat16 [4096, 1536], P(('dp', 'expert'))
- grad_gate: float32 [4096], P(('dp', 'expert'))
- grad_expert_in: bfloat16 [16, 1536, 6144], P('expert', None, 'dp')
- grad_expert_out: bfloat16 [16, 6144, 1536], P('expert', 'dp')
- grad_residual_in: bfloat16 [1536, 3072], P(None, 'dp')
- grad_residual_out: bfloat16 [3072, 1536], P('dp')
The draws below stay inside these ranges and needn't reach their ends.
Inputs may be any that keep to these rules, and one draw needn't show every extreme that they name: `expert_index`: on every device, at least 12 tokens choose one expert, the same expert on all devices, and the tokens in its first 10 slots are not dropped. `slot_index`: on each device the tokens of one expert hold the slots 0 to n - 1 once each, n being their count; dropped tokens take the highest slots of their expert; on some device all tokens choose one expert.
All inputs are finite; a program needn't handle non-finite values.
Results may differ from the reference program's by a relative error of at most 0.018.
Values may be sent and summed in bfloat16 or wider, within the bound.
A program may use at most 192 MiB of HBM per device.

```python
import jax
import jax.numpy as jnp
from jax import lax

D = 1536
FF_EXP = 6144
FF_RES = 3072
TOK_DEV = 128
EXPERTS = 16
CAP = 10
TOKENS = 4096
N_DP = 4
N_EXPERT = 8


def routing(base_key):
    favored = jax.random.randint(jax.random.fold_in(base_key, 7), (), 0, EXPERTS)
    block_count = TOKENS // TOK_DEV
    crowded = jax.random.randint(jax.random.fold_in(base_key, 13), (), 0, block_count)

    def one_block(block_index):
        block_key = jax.random.fold_in(jax.random.fold_in(base_key, 11), block_index)
        subkeys = jax.random.split(block_key, 4)
        others = jax.random.randint(subkeys[0], (TOK_DEV,), 0, EXPERTS)
        position = jnp.arange(TOK_DEV)
        chosen = jnp.where((position < CAP + 2) | (block_index == crowded), favored, others)
        dropping = (jax.random.randint(subkeys[1], (TOK_DEV,), 0, 8) == 0) & (position >= CAP)
        priority = jax.random.permutation(subkeys[2], TOK_DEV) + jnp.where(dropping, TOK_DEV, 0)
        matching = chosen[:, None] == chosen[None, :]
        slot_rank = jnp.sum(matching & (priority[None, :] < priority[:, None]), axis=1)
        shuffle = jax.random.permutation(subkeys[3], TOK_DEV)
        return (chosen[shuffle].astype(jnp.int32), slot_rank[shuffle].astype(jnp.int32), dropping[shuffle].astype(jnp.int32))
    chosen_all, slots_all, drops_all = jax.vmap(one_block)(jnp.arange(block_count))
    return (chosen_all.reshape(-1), slots_all.reshape(-1), drops_all.reshape(-1))


def draw_expert_index(key, part):
    return routing(key)[0]


def draw_slot_index(key, part):
    return routing(key)[1]


def draw_dropped(key, part):
    return routing(key)[2]


def block_levels(rng, shape, shards, low, high):
    def one(dim, shards_of):
        heights = jax.random.uniform(jax.random.fold_in(jax.random.fold_in(rng, 6), dim), (shards_of,), jnp.float32, low / len(shards), high / len(shards))
        return jnp.repeat(jnp.exp(heights), shape[dim] // shards_of).reshape((-1,) + (1,) * (len(shape) - dim - 1))

    loudness = one(*shards[0])
    for cut in shards[1:]:
        loudness = loudness * one(*cut)
    return loudness


def bell_draw(own_key, dims, deviation, most, shards=(), kind=jnp.bfloat16):
    values = jax.random.normal(own_key, dims, jnp.float32) * deviation
    if len(shards) > 0:
        values = block_levels(own_key, dims, shards, -0.22, 0.18) * values
    return jnp.clip(values, min=-most, max=most).astype(kind)


def setup_inputs(seed: int = 0) -> dict:
    seeds = jax.random.split(jax.random.key(seed), 11)
    tokens = bell_draw(seeds[0], (TOKENS, D), 1.0, 6.0, ((0, 32),))
    gate_prob = jnp.clip(0.2 + 0.8 * jax.random.uniform(seeds[1], (TOKENS,), jnp.float32) ** block_levels(seeds[1], (TOKENS,), ((0, 32),), -0.2, 0.2), 0.2, 1.0)
    expert_index = draw_expert_index(jax.random.fold_in(seeds[10], 71), 0)
    slot_index = draw_slot_index(jax.random.fold_in(seeds[10], 71), 0)
    dropped = draw_dropped(jax.random.fold_in(seeds[10], 71), 0)
    cotangent = bell_draw(seeds[5], (TOKENS, D), 1.0, 6.0, ((0, 32),))
    expert_in = bell_draw(seeds[6], (EXPERTS, D, FF_EXP), D ** -0.5, 0.15625, ((0, 8), (2, 4)))
    expert_out = bell_draw(seeds[7], (EXPERTS, FF_EXP, D), FF_EXP ** -0.5, 0.078125, ((0, 8), (1, 4)))
    residual_in = bell_draw(seeds[8], (D, FF_RES), D ** -0.5, 0.15625, ((1, 4),))
    residual_out = bell_draw(seeds[9], (FF_RES, D), FF_RES ** -0.5, 0.109375, ((0, 4),))
    return {"tokens": tokens, "gate_prob": gate_prob, "expert_index": expert_index, "slot_index": slot_index, "dropped": dropped, "cotangent": cotangent, "expert_in": expert_in, "expert_out": expert_out, "residual_in": residual_in, "residual_out": residual_out}


def gelu_tanh(values):
    return jax.nn.gelu(values, approximate=True)

def sliced_sum(left, right):
    piece_width = left.shape[1] // N_DP
    running = jnp.zeros((left.shape[0], right.shape[1]), jnp.float32)
    for piece_index in range(N_DP):
        start_col = piece_index * piece_width
        partial_term = jnp.dot(left[:, start_col:start_col + piece_width], right[start_col:start_col + piece_width], preferred_element_type=jnp.float32).astype(jnp.bfloat16)
        running = running + lax.optimization_barrier(partial_term).astype(jnp.float32)
    return running

def reference(tokens, gate_prob, expert_index, slot_index, dropped, cotangent, expert_in, expert_out, residual_in, residual_out):
    kept = (dropped == 0) & (slot_index < CAP)
    kept_float = kept.astype(jnp.float32)
    gate_kept = gate_prob * kept_float
    device_rows = N_DP * N_EXPERT * CAP
    source = (jnp.arange(TOKENS) // TOK_DEV).astype(jnp.int32)
    position = jnp.where(kept, expert_index * device_rows + source * CAP + slot_index, EXPERTS * device_rows).astype(jnp.int32)

    def place_rows(values):
        buffer = jnp.zeros((EXPERTS * device_rows + 1, D), jnp.bfloat16)
        return buffer.at[position].set(values)[:-1].reshape(EXPERTS, device_rows, D)

    def fetch_rows(buffer):
        padded = jnp.concatenate([buffer.reshape(-1, D), jnp.zeros((1, D), jnp.bfloat16)], axis=0)
        return padded[position]
    column = place_rows(tokens)
    scaled = (cotangent.astype(jnp.float32) * gate_kept[:, None]).astype(jnp.bfloat16)
    grad_column = place_rows(scaled)

    def per_expert(operands):
        rows_block, grad_block, weight_in, weight_out = operands
        pre_act = jnp.dot(rows_block, weight_in, preferred_element_type=jnp.float32)
        hidden_f, gelu_back = jax.vjp(gelu_tanh, pre_act)
        hidden = hidden_f.astype(jnp.bfloat16)
        result = sliced_sum(hidden, weight_out).astype(jnp.bfloat16)
        grad_hidden = jnp.dot(grad_block, weight_out.T, preferred_element_type=jnp.float32)
        grad_pre = gelu_back(grad_hidden)[0].astype(jnp.bfloat16)
        grad_out = jnp.dot(hidden.T, grad_block, preferred_element_type=jnp.float32).astype(jnp.bfloat16)
        grad_in = jnp.dot(rows_block.T, grad_pre, preferred_element_type=jnp.float32).astype(jnp.bfloat16)
        grad_rows = sliced_sum(grad_pre, weight_in.T).astype(jnp.bfloat16)
        return (result, grad_rows, grad_in, grad_out)
    results, grad_rows, grad_in, grad_out = lax.map(per_expert, (column, grad_column, expert_in, expert_out))
    expert_token = fetch_rows(results).astype(jnp.float32)
    pre_dense = jnp.dot(tokens, residual_in, preferred_element_type=jnp.float32)
    dense_f, dense_back = jax.vjp(gelu_tanh, pre_dense)
    dense_hidden = dense_f.astype(jnp.bfloat16)
    dense_sum = sliced_sum(dense_hidden, residual_out)
    output = (dense_sum + gate_kept[:, None] * expert_token).astype(jnp.bfloat16)
    grad_gate = kept_float * lax.optimization_barrier(jnp.sum(cotangent.astype(jnp.float32) * expert_token, axis=1))
    dense_grad_hidden = jnp.dot(cotangent, residual_out.T, preferred_element_type=jnp.float32)
    dense_grad_pre = dense_back(dense_grad_hidden)[0].astype(jnp.bfloat16)
    grad_res_out = jnp.dot(dense_hidden.T, cotangent, preferred_element_type=jnp.float32).astype(jnp.bfloat16)
    grad_res_in = jnp.dot(tokens.T, dense_grad_pre, preferred_element_type=jnp.float32).astype(jnp.bfloat16)
    dense_dx = sliced_sum(dense_grad_pre, residual_in.T)
    grad_tokens = (dense_dx + fetch_rows(grad_rows).astype(jnp.float32)).astype(jnp.bfloat16)
    return (output, grad_tokens, grad_gate, grad_in, grad_out, grad_res_in, grad_res_out)
```

```python
import functools

import jax
import jax.numpy as jnp
import numpy as np
from jax import lax
from jax.experimental import pallas as pl
from jax.experimental.pallas import tpu as pltpu
from jax.sharding import PartitionSpec as P

MESH = pl.DeviceIdType.MESH
F32 = jnp.float32
BF16 = jnp.bfloat16
GELU_C = float(np.sqrt(2.0 / np.pi))


def mm(left, right, left_dim=1, right_dim=0):
    return lax.dot_general(
        left, right, (((left_dim,), (right_dim,)), ((), ())), preferred_element_type=F32
    )


def gelu_parts(v):
    square = v * v
    t = jnp.tanh(GELU_C * (v + 0.044715 * (square * v)))
    half = 0.5 * (1.0 + t)
    slope = half + (0.5 * v) * (1.0 - t * t) * (GELU_C * (1.0 + (3 * 0.044715) * square))
    return v * half, slope


def tile_of(size, want):
    while size % want:
        want //= 2
    return want


def tiles(size, want, body):
    step = tile_of(size, want)

    def one(i, carry):
        body(pl.ds(pl.multiple_of(i * step, step), step))
        return carry

    lax.fori_loop(0, size // step, one, 0)


def greet(dp_count, host_count):
    dp, ex = lax.axis_index("dp"), lax.axis_index("expert")
    barrier = pltpu.get_barrier_semaphore()
    for k in range(1, dp_count):
        pl.semaphore_signal(
            barrier, inc=1, device_id=(lax.rem(dp + k, dp_count), ex), device_id_type=MESH
        )
    for k in range(1, host_count):
        pl.semaphore_signal(
            barrier, inc=1, device_id=(dp, lax.rem(ex + k, host_count)), device_id_type=MESH
        )
    pl.semaphore_wait(barrier, dp_count - 1 + host_count - 1)
    return dp, ex


def gather_kernel(
    n, hosts,
    tok, cot, sendbuf, perm, rin_hbm, rout_hbm,
    column, partial, gin, gout,
    rin, rout, rows, arrived, slab, hid, gpre,
    wsem, lsem, dsend, drecv, asend, arecv, csend, crecv,
):
    w0 = pltpu.make_async_copy(rin_hbm, rin, wsem.at[0])
    w1 = pltpu.make_async_copy(rout_hbm, rout, wsem.at[1])
    w0.start()
    w1.start()
    dp, ex = greet(n, hosts)
    dense = []
    for a, src in enumerate((tok, cot)):
        for k in range(1, n):
            to = lax.rem(dp + k, n)
            c = pltpu.make_async_remote_copy(
                src_ref=src, dst_ref=rows.at[a, dp],
                send_sem=dsend.at[a, k - 1], recv_sem=drecv.at[a, k - 1],
                device_id=(to, ex), device_id_type=MESH,
            )
            c.start()
            dense.append(c)
        if a == 0:
            a2a = []
            for k in range(1, hosts):
                to = lax.rem(ex + k, hosts)
                c = pltpu.make_async_remote_copy(
                    src_ref=sendbuf.at[to], dst_ref=arrived.at[ex],
                    send_sem=asend.at[k - 1], recv_sem=arecv.at[k - 1],
                    device_id=(dp, to), device_id_type=MESH,
                )
                c.start()
                a2a.append(c)
    arrived[ex] = sendbuf[ex]
    rows[0, dp] = tok[...]
    rows[1, dp] = cot[...]
    for c in a2a:
        c.wait_recv()
    hr = arrived.shape[0] * arrived.shape[1]
    width = arrived.shape[2]

    def place(cols):
        got = arrived[:, :, cols].reshape(hr, cols.size)
        slab[:, cols] = mm(perm[...], got).astype(BF16)

    tiles(width, 512, place)
    local = pltpu.make_async_copy(slab, column.at[dp], lsem)
    local.start()
    col = []
    for k in range(1, n):
        to = lax.rem(dp + k, n)
        c = pltpu.make_async_remote_copy(
            src_ref=slab, dst_ref=column.at[dp],
            send_sem=csend.at[k - 1], recv_sem=crecv.at[k - 1],
            device_id=(to, ex), device_id_type=MESH,
        )
        c.start()
        col.append(c)
    w0.wait()
    w1.wait()
    for c in dense:
        c.wait_recv()
    tokens_all = n * tok.shape[0]
    hidden = rin.shape[1]

    def units(f):
        x = rows[0].reshape(tokens_all, width)
        g = rows[1].reshape(tokens_all, width)
        value, slope = gelu_parts(mm(x, rin[:, f]))
        h = value.astype(BF16)
        hid[:, f] = h
        p = (slope * mm(g, rout[f, :], 1, 1)).astype(BF16)
        gpre[:, f] = p
        gout[f, :] = mm(h, g, 0, 0).astype(BF16)
        gin[:, f] = mm(x, p, 0, 0).astype(BF16)

    tiles(hidden, 256, units)

    def back(d):
        o = mm(hid[...], rout[:, d]).astype(BF16)
        partial[0, :, :, d] = o.reshape(n, tok.shape[0], d.size)
        o = mm(gpre[...], rin[d, :], 1, 1).astype(BF16)
        partial[1, :, :, d] = o.reshape(n, tok.shape[0], d.size)

    tiles(width, 256, back)
    local.wait()
    for c in col:
        c.wait()
    for c in dense + a2a:
        c.wait_send()


def expert_kernel(
    n, hosts, local_count,
    cot, gate, kept, pick, unperm, partial, column, win_hbm, wout_hbm,
    output, grad_tokens, grad_gate, hid_out, gpre_out,
    win, wout, colv, hid, gpre, part, drecv_buf, own_dense, erecv_buf, sendback, back,
    wsem, csem, osem, dsend, drecv, esend, erecv, bsend, brecv, hsem,
):
    loads = []
    for j in range(local_count):
        c0 = pltpu.make_async_copy(win_hbm.at[j], win.at[j], wsem.at[j, 0])
        c1 = pltpu.make_async_copy(wout_hbm.at[j], wout.at[j], wsem.at[j, 1])
        cs = [
            pltpu.make_async_copy(column.at[:, a * local_count + j], colv.at[a, j], csem.at[j, a])
            for a in range(2)
        ]
        for c in [cs[0], c0, cs[1], c1]:
            c.start()
        loads.append([c0, c1] + cs)
    dp, ex = greet(n, hosts)
    dense = []
    for a in range(2):
        for k in range(1, n):
            to = lax.rem(dp + k, n)
            c = pltpu.make_async_remote_copy(
                src_ref=partial.at[a, to], dst_ref=drecv_buf.at[a, k - 1],
                send_sem=dsend.at[a, k - 1], recv_sem=drecv.at[a, k - 1],
                device_id=(to, ex), device_id_type=MESH,
            )
            c.start()
            dense.append(c)
    own = pltpu.make_async_copy(partial.at[:, dp], own_dense, osem)
    own.start()
    slots, width = colv.shape[3], colv.shape[4]
    all_rows = n * slots
    units = win.shape[2]
    scatter = [[], []]
    saves = []

    def push(a, j):
        for k in range(1, n):
            to = lax.rem(dp + k, n)
            c = pltpu.make_async_remote_copy(
                src_ref=part.at[a, j, to], dst_ref=erecv_buf.at[a, j, k - 1],
                send_sem=esend.at[a, j, k - 1], recv_sem=erecv.at[a, j, k - 1],
                device_id=(to, ex), device_id_type=MESH,
            )
            c.start()
            scatter[a].append(c)

    for j in range(local_count):
        for c in loads[j]:
            c.wait()

        def forward(f):
            x = colv[0, j].reshape(all_rows, width)
            g = colv[1, j].reshape(all_rows, width)
            value, slope = gelu_parts(mm(x, win[j, :, f]))
            hid[j, :, f] = value.astype(BF16)
            gpre[j, :, f] = (slope * mm(g, wout[j, f, :], 1, 1)).astype(BF16)

        tiles(units, 256, forward)

        def project(d):
            o = mm(hid[j], wout[j, :, d]).astype(BF16)
            part[0, j, :, :, d] = o.reshape(n, slots, d.size)

        tiles(width, 256, project)
        push(0, j)

        def project_back(d):
            o = mm(gpre[j], win[j, d, :], 1, 1).astype(BF16)
            part[1, j, :, :, d] = o.reshape(n, slots, d.size)

        tiles(width, 256, project_back)
        push(1, j)
        for s, (src, dst) in enumerate(((hid, hid_out), (gpre, gpre_out))):
            c = pltpu.make_async_copy(src.at[j], dst.at[j], hsem.at[j, s])
            c.start()
            saves.append(c)

    back_copies = [[], []]
    hr = back.shape[1] * back.shape[2]
    for a in range(2):
        for c in scatter[a]:
            c.wait_recv()

        def collect(d):
            total = part[a, :, dp, :, d].astype(F32)
            for k in range(n - 1):
                total = total + erecv_buf[a, :, k, :, d].astype(F32)
            summed = total.astype(BF16).reshape(local_count * slots, d.size)
            o = mm(unperm[...], summed).astype(BF16)
            sendback[a, :, :, d] = o.reshape(back.shape[1], back.shape[2], d.size)

        tiles(width, 256, collect)
        for k in range(1, hosts):
            to = lax.rem(ex + k, hosts)
            c = pltpu.make_async_remote_copy(
                src_ref=sendback.at[a, to], dst_ref=back.at[a, ex],
                send_sem=bsend.at[a, k - 1], recv_sem=brecv.at[a, k - 1],
                device_id=(dp, to), device_id_type=MESH,
            )
            c.start()
            back_copies[a].append(c)
        back[a, ex] = sendback[a, ex]
    own.wait()
    for c in dense:
        c.wait_recv()

    for a in range(2):
        for c in back_copies[a]:
            c.wait_recv()

        for lo in range(0, width, tile_of(width, 512)):
            d = pl.ds(lo, tile_of(width, 512))
            total = own_dense[a, :, d].astype(F32)
            for k in range(n - 1):
                total = total + drecv_buf[a, k, :, d].astype(F32)
            mine = mm(pick[...], back[a, :, :, d].reshape(hr, d.size))
            if a == 0:
                output[:, d] = (total + gate[...] * mine).astype(BF16)
                term = jnp.sum(cot[:, d].astype(F32) * mine, axis=1, keepdims=True)
                gg = term if lo == 0 else gg + term
            else:
                grad_tokens[:, d] = (total + mine).astype(BF16)
        if a == 0:
            grad_gate[...] = kept[...] * gg
    for c in saves:
        c.wait()
    for c in dense + scatter[0] + scatter[1] + back_copies[0] + back_copies[1]:
        c.wait_send()


def ceil16(v):
    return -(-v // 16) * 16


def on_device(
    tokens, gate_prob, expert_index, slot_index, dropped, cotangent,
    expert_in, expert_out, residual_in, residual_out,
):
    n = lax.axis_size("dp")
    hosts = lax.axis_size("expert")
    local_count, width, units = expert_in.shape
    hidden = residual_in.shape[1]
    experts_all = local_count * hosts
    row_count = tokens.shape[0]
    capacity = max(2, 5 * row_count // (4 * experts_all))
    kept = (dropped == 0) & (slot_index < capacity)
    kept_float = kept.astype(F32)
    gate_kept = gate_prob * kept_float
    block = local_count * capacity
    send_rows = ceil16(2 * block)
    back_rows = ceil16(block)
    slots = ceil16(hosts * capacity)

    host = expert_index // local_count
    within = (expert_index % local_count) * capacity + slot_index
    send_pos = jnp.where(kept, host * send_rows + within, -1)
    back_pos = jnp.where(kept, host * back_rows + within, -1)
    scaled = (cotangent.astype(F32) * gate_kept[:, None]).astype(BF16)
    target = jnp.arange(hosts * send_rows, dtype=jnp.int32)[:, None]
    grad_pos = jnp.where(kept, send_pos + block, -1)
    place = jnp.concatenate(
        [(target == send_pos[None]).astype(BF16), (target == grad_pos[None]).astype(BF16)], axis=1
    )
    sendbuf = mm(place, jnp.concatenate([tokens, scaled], axis=0)).astype(BF16)
    sendbuf = sendbuf.reshape(hosts, send_rows, width)
    pick = (jnp.arange(hosts * back_rows, dtype=jnp.int32)[None] == back_pos[:, None]).astype(BF16)

    perm = np.zeros((2, local_count, slots, hosts, send_rows), np.float32)
    unperm = np.zeros((hosts, back_rows, local_count, slots), np.float32)
    for j in range(local_count):
        for h in range(hosts):
            for c in range(capacity):
                unperm[h, j * capacity + c, j, h * capacity + c] = 1
                for a in range(2):
                    perm[a, j, h * capacity + c, h, a * block + j * capacity + c] = 1
    perm = jnp.asarray(perm.reshape(2 * local_count * slots, hosts * send_rows), BF16)
    unperm = jnp.asarray(unperm.reshape(hosts * back_rows, local_count * slots), BF16)

    vmem = pl.BlockSpec(memory_space=pltpu.VMEM)
    anyspace = pl.BlockSpec(memory_space=pl.ANY)
    dma = pltpu.SemaphoreType.DMA
    tokens_all = n * row_count
    column, partial, gin, gout = pl.pallas_call(
        functools.partial(gather_kernel, n, hosts),
        out_shape=(
            jax.ShapeDtypeStruct((n, 2 * local_count * slots, width), BF16),
            jax.ShapeDtypeStruct((2, n, row_count, width), BF16),
            jax.ShapeDtypeStruct((width, hidden), BF16),
            jax.ShapeDtypeStruct((hidden, width), BF16),
        ),
        in_specs=[vmem, vmem, vmem, vmem, anyspace, anyspace],
        out_specs=(anyspace, vmem, vmem, vmem),
        scratch_shapes=[
            pltpu.VMEM((width, hidden), BF16),
            pltpu.VMEM((hidden, width), BF16),
            pltpu.VMEM((2, n, row_count, width), BF16),
            pltpu.VMEM((hosts, send_rows, width), BF16),
            pltpu.VMEM((2 * local_count * slots, width), BF16),
            pltpu.VMEM((tokens_all, hidden), BF16),
            pltpu.VMEM((tokens_all, hidden), BF16),
            dma((2,)),
            dma,
            dma((2, n - 1)),
            dma((2, n - 1)),
            dma((hosts - 1,)),
            dma((hosts - 1,)),
            dma((n - 1,)),
            dma((n - 1,)),
        ],
        compiler_params=pltpu.CompilerParams(
            collective_id=0, has_side_effects=True, vmem_limit_bytes=56 * 2**20
        ),
        name="gather_dense",
    )(tokens, cotangent, sendbuf, perm, residual_in, residual_out)

    in_total, out_total = lax.psum((gin, gout), "expert")

    column = column.reshape(n, 2 * local_count, slots, width)
    all_rows = n * slots
    output, grad_tokens, grad_gate, hid, gpre = pl.pallas_call(
        functools.partial(expert_kernel, n, hosts, local_count),
        out_shape=(
            jax.ShapeDtypeStruct((row_count, width), BF16),
            jax.ShapeDtypeStruct((row_count, width), BF16),
            jax.ShapeDtypeStruct((row_count, 1), F32),
            jax.ShapeDtypeStruct((local_count, all_rows, units), BF16),
            jax.ShapeDtypeStruct((local_count, all_rows, units), BF16),
        ),
        in_specs=[vmem] * 5 + [anyspace] * 4,
        out_specs=(vmem, vmem, vmem, anyspace, anyspace),
        scratch_shapes=[
            pltpu.VMEM((local_count, width, units), BF16),
            pltpu.VMEM((local_count, units, width), BF16),
            pltpu.VMEM((2, local_count, n, slots, width), BF16),
            pltpu.VMEM((local_count, all_rows, units), BF16),
            pltpu.VMEM((local_count, all_rows, units), BF16),
            pltpu.VMEM((2, local_count, n, slots, width), BF16),
            pltpu.VMEM((2, n - 1, row_count, width), BF16),
            pltpu.VMEM((2, row_count, width), BF16),
            pltpu.VMEM((2, local_count, n - 1, slots, width), BF16),
            pltpu.VMEM((2, hosts, back_rows, width), BF16),
            pltpu.VMEM((2, hosts, back_rows, width), BF16),
            dma((local_count, 2)),
            dma((local_count, 2)),
            dma,
            dma((2, n - 1)),
            dma((2, n - 1)),
            dma((2, local_count, n - 1)),
            dma((2, local_count, n - 1)),
            dma((2, hosts - 1)),
            dma((2, hosts - 1)),
            dma((local_count, 2)),
        ],
        compiler_params=pltpu.CompilerParams(
            collective_id=1, has_side_effects=True, vmem_limit_bytes=60 * 2**20
        ),
        name="expert_scatter",
    )(
        cotangent, gate_kept[:, None], kept_float[:, None], pick, unperm,
        partial, column, expert_in, expert_out,
    )

    grad_expert_out = jnp.einsum(
        "jnsf,njsd->jfd", hid.reshape(local_count, n, slots, units), column[:, local_count:],
        preferred_element_type=F32,
    ).astype(BF16)
    grad_expert_in = jnp.einsum(
        "njsd,jnsf->jdf", column[:, :local_count], gpre.reshape(local_count, n, slots, units),
        preferred_element_type=F32,
    ).astype(BF16)
    return (
        output,
        grad_tokens,
        grad_gate[:, 0],
        grad_expert_in,
        grad_expert_out,
        in_total,
        out_total,
    )


def solution(mesh):
    return jax.shard_map(
        on_device,
        mesh=mesh,
        in_specs=(
            P(("dp", "expert"), None),
            P(("dp", "expert")),
            P(("dp", "expert")),
            P(("dp", "expert")),
            P(("dp", "expert")),
            P(("dp", "expert"), None),
            P("expert", None, "dp"),
            P("expert", "dp", None),
            P(None, "dp"),
            P("dp", None),
        ),
        out_specs=(
            P(("dp", "expert"), None),
            P(("dp", "expert"), None),
            P(("dp", "expert")),
            P("expert", None, "dp"),
            P("expert", "dp", None),
            P(None, "dp"),
            P("dp", None),
        ),
        check_vma=False,
    )
```

```python
import functools

import jax
import jax.numpy as jnp
import numpy as np
from jax import lax
from jax.experimental import pallas as pl
from jax.experimental.pallas import tpu as pltpu
from jax.sharding import PartitionSpec as P

MESH = pl.DeviceIdType.MESH
F32 = jnp.float32
BF16 = jnp.bfloat16
GELU_C = float(np.sqrt(2.0 / np.pi))


def mm(left, right, left_dim=1, right_dim=0):
    return lax.dot_general(
        left, right, (((left_dim,), (right_dim,)), ((), ())), preferred_element_type=F32
    )


def gelu_parts(v):
    square = v * v
    t = jnp.tanh(GELU_C * (v + 0.044715 * (square * v)))
    half = 0.5 * (1.0 + t)
    slope = half + (0.5 * v) * (1.0 - t * t) * (GELU_C * (1.0 + (3 * 0.044715) * square))
    return v * half, slope


def tile_of(size, want):
    while size % want:
        want //= 2
    return want


def tiles(size, want, body):
    step = tile_of(size, want)

    def one(i, carry):
        body(pl.ds(pl.multiple_of(i * step, step), step))
        return carry

    lax.fori_loop(0, size // step, one, 0)


def greet(dp_count, host_count):
    dp, ex = lax.axis_index("dp"), lax.axis_index("expert")
    barrier = pltpu.get_barrier_semaphore()
    for k in range(1, dp_count):
        pl.semaphore_signal(
            barrier, inc=1, device_id=(lax.rem(dp + k, dp_count), ex), device_id_type=MESH
        )
    for k in range(1, host_count):
        pl.semaphore_signal(
            barrier, inc=1, device_id=(dp, lax.rem(ex + k, host_count)), device_id_type=MESH
        )
    pl.semaphore_wait(barrier, dp_count - 1 + host_count - 1)
    return dp, ex


def layer_kernel(
    n, hosts, local_count, reduce_here,
    tok, cot, sendbuf, perm, gate, kept, pick, unperm, rin_hbm, rout_hbm, win_hbm, wout_hbm,
    output, grad_tokens, grad_gate, gin, gout, gwin, gwout,
    rin, rout, rows, arrived, colv, dhid, dgpre, partial, pin, pout, in1, out1, in2, out2,
    win, wout, hid, gpre, part, drecv_buf, erecv_buf, back,
    wsem, gsem, asend, arecv, bsend, brecv, hsend, hrecv, dsend, drecv, esend, erecv,
    csend, crecv, psend, precv, qsend, qrecv, ssend, srecv, lsem,
):
    loads = [pltpu.make_async_copy(rin_hbm, rin, wsem.at[0, 0]),
             pltpu.make_async_copy(rout_hbm, rout, wsem.at[0, 1])]
    for j in range(local_count):
        loads.append(pltpu.make_async_copy(win_hbm.at[j], win.at[j], wsem.at[1 + j, 0]))
        loads.append(pltpu.make_async_copy(wout_hbm.at[j], wout.at[j], wsem.at[1 + j, 1]))
    for c in loads:
        c.start()
    dp, ex = greet(n, hosts)
    sends = []

    def remote(src, dst, send_sem, recv_sem, to):
        c = pltpu.make_async_remote_copy(
            src_ref=src, dst_ref=dst, send_sem=send_sem, recv_sem=recv_sem,
            device_id=to, device_id_type=MESH,
        )
        c.start()
        sends.append(c)
        return c

    square = n == 4
    beside = lax.div(dp, 2) * 2 + 1 - lax.rem(dp, 2) if square else None
    across = lax.rem(dp + 2, n) if square else None

    def spread(srcs, buf, ssem, rsem):
        if not square:
            return [
                [remote(srcs[a], buf.at[a, dp], ssem.at[a, k - 1], rsem.at[a, k - 1],
                        (lax.rem(dp + k, n), ex)) for k in range(1, n)]
                for a in range(2)
            ]
        return [
            [remote(srcs[a], buf.at[a, dp], ssem.at[a, k], rsem.at[a, k], (to, ex))
             for k, to in enumerate((beside, across))]
            for a in range(2)
        ]

    def relay(copies, buf, ssem, rsem):
        if not square:
            return [c for pair in copies for c in pair]
        copies[0][1].wait_recv()
        f0 = remote(buf.at[0, across], buf.at[0, across], ssem.at[0, 2], rsem.at[0, 2], (beside, ex))
        copies[1][0].wait_recv()
        f1 = remote(buf.at[1, beside], buf.at[1, beside], ssem.at[1, 2], rsem.at[1, 2], (across, ex))
        return [copies[0][0], copies[1][1], f0, f1]

    row_count, width = tok.shape
    tokens_all = n * row_count
    hidden = rin.shape[1]
    rows[0, dp] = tok[...]
    rows[1, dp] = cot[...]
    dense = spread((tok, cot), rows, asend, arecv)
    a2a = [
        remote(sendbuf.at[to], arrived.at[ex], bsend.at[k - 1], brecv.at[k - 1], (dp, to))
        for k, to in ((k, lax.rem(ex + k, hosts)) for k in range(1, hosts))
    ]
    keep = pltpu.make_async_copy(sendbuf.at[ex], arrived.at[ex], lsem.at[2])
    keep.start()
    rest = relay(dense, rows, asend, arecv)
    mark = len(sends)
    for c in a2a:
        c.wait_recv()
    keep.wait()
    hr = arrived.shape[0] * arrived.shape[1]
    slots = colv.shape[3]

    def place(cols):
        got = arrived[:, :, cols].reshape(hr, cols.size)
        put = mm(perm[...], got).astype(BF16)
        colv[:, dp, :, :, cols] = put.reshape(2, local_count, slots, cols.size)

    tiles(width, 512, place)
    column = spread((colv.at[0, dp], colv.at[1, dp]), colv, hsend, hrecv)
    loads[0].wait()
    loads[1].wait()
    for c in rest:
        c.wait_recv()

    def dense_units(f):
        x = rows[0].reshape(tokens_all, width)
        g = rows[1].reshape(tokens_all, width)
        value, slope = gelu_parts(mm(x, rin[:, f]))
        h = value.astype(BF16)
        dhid[:, f] = h
        p = (slope * mm(g, rout[f, :], 1, 1)).astype(BF16)
        dgpre[:, f] = p
        pout[f, :] = mm(h, g, 0, 0).astype(BF16)
        pin[:, f] = mm(x, p, 0, 0).astype(BF16)

    tiles(hidden, 256, dense_units)

    chips = hosts // 2
    chip, core = lax.div(ex, 2), lax.rem(ex, 2)
    other = 1 - core
    sibling = chip * 2 + other
    pairs = ((pin, in1, in2, rin, gin), (pout, out1, out2, rout, gout))

    def block_of(ref, c, q):
        size = ref.shape[0] // hosts
        return pl.ds(pl.multiple_of((c * chips + q) * size, 16), size)

    def half_of(ref, c):
        size = ref.shape[0] // 2
        return pl.ds(pl.multiple_of(c * size, 16), size)

    if reduce_here:
        first = [
            remote(p.at[half_of(p, other)], r1, psend.at[i], precv.at[i], (dp, sibling))
            for i, (p, r1, r2, s, o) in enumerate(pairs)
        ]

    def dense_back(d):
        o = mm(dhid[...], rout[:, d]).astype(BF16)
        partial[0, :, :, d] = o.reshape(n, row_count, d.size)
        o = mm(dgpre[...], rin[d, :], 1, 1).astype(BF16)
        partial[1, :, :, d] = o.reshape(n, row_count, d.size)

    tiles(width, 256, dense_back)
    second = []
    if reduce_here:
        for i, (p, r1, r2, s, o) in enumerate(pairs):
            first[i].wait_recv()
            size = p.shape[0] // hosts
            for q in range(chips):
                at = pl.ds(q * size, size)
                s[at, :] = (p[block_of(p, core, q), :].astype(F32) + r1[at, :].astype(F32)).astype(BF16)
            for k in range(1, chips):
                q = lax.rem(chip + k, chips)
                second.append(remote(
                    s.at[pl.ds(pl.multiple_of(q * size, 16), size)], r2.at[k - 1],
                    psend.at[2 + i * (chips - 1) + k - 1], precv.at[2 + i * (chips - 1) + k - 1],
                    (dp, q * 2 + core),
                ))
    else:
        saves = [pltpu.make_async_copy(pin, gin, lsem.at[0]), pltpu.make_async_copy(pout, gout, lsem.at[1])]
        for c in saves:
            c.start()
    rest = relay(column, colv, hsend, hrecv)
    dense_rs = [
        remote(partial.at[a, to], drecv_buf.at[a, k - 1], dsend.at[a, k - 1], drecv.at[a, k - 1], (to, ex))
        for a in range(2) for k, to in ((k, lax.rem(dp + k, n)) for k in range(1, n))
    ]
    for c in rest:
        c.wait_recv()

    all_rows = n * slots
    units = win.shape[2]
    scatter = [[], []]

    def push(a, j):
        for k in range(1, n):
            to = lax.rem(dp + k, n)
            scatter[a].append(remote(
                part.at[a, j, to], erecv_buf.at[a, j, k - 1],
                esend.at[a, j, k - 1], erecv.at[a, j, k - 1], (to, ex),
            ))

    for j in range(local_count):
        loads[2 + 2 * j].wait()
        loads[3 + 2 * j].wait()

        def forward(f):
            x = colv[0, :, j].reshape(all_rows, width)
            g = colv[1, :, j].reshape(all_rows, width)
            value, slope = gelu_parts(mm(x, win[j, :, f]))
            hid[j, :, f] = value.astype(BF16)
            gpre[j, :, f] = (slope * mm(g, wout[j, f, :], 1, 1)).astype(BF16)

        tiles(units, 256, forward)

        def project(d):
            o = mm(hid[j], wout[j, :, d]).astype(BF16)
            part[0, j, :, :, d] = o.reshape(n, slots, d.size)

        tiles(width, 256, project)
        push(0, j)

        def project_back(d):
            o = mm(gpre[j], win[j, d, :], 1, 1).astype(BF16)
            part[1, j, :, :, d] = o.reshape(n, slots, d.size)

        tiles(width, 256, project_back)
        push(1, j)

    third = []
    if reduce_here:
        saves = []
        for c in second:
            c.wait_recv()
        for i, (p, r1, r2, s, o) in enumerate(pairs):
            size = p.shape[0] // hosts
            total = s[pl.ds(pl.multiple_of(chip * size, 16), size), :].astype(F32)
            for k in range(chips - 1):
                total = total + r2[k].astype(F32)
            done = s.at[pl.ds(chips * size, size)]
            done[...] = total.astype(BF16)
            c = pltpu.make_async_copy(done, o.at[block_of(o, core, chip)], lsem.at[i])
            c.start()
            saves.append(c)
            for k in range(1, chips):
                q = lax.rem(chip + k, chips)
                third.append(remote(
                    done, o.at[block_of(o, core, chip)],
                    qsend.at[i, k - 1], qrecv.at[i, k - 1], (dp, q * 2 + core),
                ))

    grads = []
    for j in range(local_count):

        def weights(f):
            g = colv[1, :, j].reshape(all_rows, width)
            wout[j, f, :] = mm(hid[j, :, f], g, 0, 0).astype(BF16)
            x = colv[0, :, j].reshape(all_rows, width)
            win[j, :, f] = mm(x, gpre[j, :, f], 0, 0).astype(BF16)

        tiles(units, 256, weights)
        for s, (src, dst) in enumerate(((win, gwin), (wout, gwout))):
            c = pltpu.make_async_copy(src.at[j], dst.at[j], gsem.at[j, s])
            c.start()
            grads.append(c)

    back_rows = back.shape[2]
    back_all = hosts * back_rows
    back_copies = [[], []]
    per = row_count // back_rows

    def rows_for(a, host):
        start = pl.multiple_of(lax.rem(host, per) * back_rows, back_rows)
        return rows.at[a, lax.div(host, per), pl.ds(start, back_rows)]

    for c in sends[:mark]:
        c.wait_send()
    for a in range(2):
        for c in scatter[a]:
            c.wait_recv()

        def collect(d):
            total = part[a, :, dp, :, d].astype(F32)
            for k in range(n - 1):
                total = total + erecv_buf[a, :, k, :, d].astype(F32)
            summed = total.astype(BF16).reshape(local_count * slots, d.size)
            o = mm(unperm[...], summed).astype(BF16)
            rows[a, :hosts // per, :, d] = o.reshape(hosts // per, row_count, d.size)

        tiles(width, 256, collect)
        for k in range(1, hosts):
            to = lax.rem(ex + k, hosts)
            back_copies[a].append(remote(
                rows_for(a, to), back.at[a, ex], csend.at[a, k - 1], crecv.at[a, k - 1], (dp, to)
            ))
        back[a, ex] = rows_for(a, ex)[...]
    fourth = []
    if reduce_here:
        for c in saves:
            c.wait()
        for c in third:
            c.wait_recv()
        for i, (p, r1, r2, s, o) in enumerate(pairs):
            fourth.append(remote(
                o.at[half_of(o, core)], o.at[half_of(o, core)], ssend.at[i], srecv.at[i], (dp, sibling)
            ))
        saves = []
    for c in dense_rs:
        c.wait_recv()

    for a in range(2):
        for c in back_copies[a]:
            c.wait_recv()
        for lo in range(0, width, tile_of(width, 512)):
            d = pl.ds(lo, tile_of(width, 512))
            total = partial[a, dp, :, d].astype(F32)
            for k in range(n - 1):
                total = total + drecv_buf[a, k, :, d].astype(F32)
            mine = mm(pick[...], back[a, :, :, d].reshape(back_all, d.size))
            if a == 0:
                output[:, d] = (total + gate[...] * mine).astype(BF16)
                term = jnp.sum(cot[:, d].astype(F32) * mine, axis=1, keepdims=True)
                gg = term if lo == 0 else gg + term
            else:
                grad_tokens[:, d] = (total + mine).astype(BF16)
        if a == 0:
            grad_gate[...] = kept[...] * gg
    for c in grads + saves:
        c.wait()
    for c in fourth:
        c.wait_recv()
    for c in sends[mark:]:
        c.wait_send()


def ceil16(v):
    return -(-v // 16) * 16


def on_device(
    tokens, gate_prob, expert_index, slot_index, dropped, cotangent,
    expert_in, expert_out, residual_in, residual_out,
):
    n = lax.axis_size("dp")
    hosts = lax.axis_size("expert")
    local_count, width, units = expert_in.shape
    hidden = residual_in.shape[1]
    experts_all = local_count * hosts
    row_count = tokens.shape[0]
    capacity = max(2, 5 * row_count // (4 * experts_all))
    kept = (dropped == 0) & (slot_index < capacity)
    kept_float = kept.astype(F32)
    gate_kept = gate_prob * kept_float
    block = local_count * capacity
    send_rows = ceil16(2 * block)
    back_rows = ceil16(block)
    slots = ceil16(hosts * capacity)

    host = expert_index // local_count
    within = (expert_index % local_count) * capacity + slot_index
    send_pos = jnp.where(kept, host * send_rows + within, -1)
    back_pos = jnp.where(kept, host * back_rows + within, -1)
    scaled = (cotangent.astype(F32) * gate_kept[:, None]).astype(BF16)
    target = jnp.arange(hosts * send_rows, dtype=jnp.int32)[:, None]
    grad_pos = jnp.where(kept, send_pos + block, -1)
    place = jnp.concatenate(
        [(target == send_pos[None]).astype(BF16), (target == grad_pos[None]).astype(BF16)], axis=1
    )
    sendbuf = mm(place, jnp.concatenate([tokens, scaled], axis=0)).astype(BF16)
    sendbuf = sendbuf.reshape(hosts, send_rows, width)
    pick = (jnp.arange(hosts * back_rows, dtype=jnp.int32)[None] == back_pos[:, None]).astype(BF16)

    perm = np.zeros((2, local_count, slots, hosts, send_rows), np.float32)
    unperm = np.zeros((hosts, back_rows, local_count, slots), np.float32)
    for j in range(local_count):
        for h in range(hosts):
            for c in range(capacity):
                unperm[h, j * capacity + c, j, h * capacity + c] = 1
                for a in range(2):
                    perm[a, j, h * capacity + c, h, a * block + j * capacity + c] = 1
    perm = jnp.asarray(perm.reshape(2 * local_count * slots, hosts * send_rows), BF16)
    unperm = jnp.asarray(unperm.reshape(hosts * back_rows, local_count * slots), BF16)

    vmem = pl.BlockSpec(memory_space=pltpu.VMEM)
    anyspace = pl.BlockSpec(memory_space=pl.ANY)
    dma = pltpu.SemaphoreType.DMA
    all_rows = n * slots
    reduce_here = hosts % 2 == 0 and width % (16 * hosts) == 0 and hidden % (16 * hosts) == 0
    chips = hosts // 2
    reduce_shapes = (
        (width // 2, hidden),
        (hidden // 2, width),
        (chips - 1, width // hosts, hidden),
        (chips - 1, hidden // hosts, width),
    )
    output, grad_tokens, grad_gate, in_total, out_total, grad_expert_in, grad_expert_out = pl.pallas_call(
        functools.partial(layer_kernel, n, hosts, local_count, reduce_here),
        out_shape=(
            jax.ShapeDtypeStruct((row_count, width), BF16),
            jax.ShapeDtypeStruct((row_count, width), BF16),
            jax.ShapeDtypeStruct((row_count, 1), F32),
            jax.ShapeDtypeStruct((width, hidden), BF16),
            jax.ShapeDtypeStruct((hidden, width), BF16),
            jax.ShapeDtypeStruct((local_count, width, units), BF16),
            jax.ShapeDtypeStruct((local_count, units, width), BF16),
        ),
        in_specs=[vmem] * 2 + [anyspace] + [vmem] * 5 + [anyspace] * 4,
        out_specs=(vmem, vmem, vmem, anyspace, anyspace, anyspace, anyspace),
        scratch_shapes=[
            pltpu.VMEM((width, hidden), BF16),
            pltpu.VMEM((hidden, width), BF16),
            pltpu.VMEM((2, n, row_count, width), BF16),
            pltpu.VMEM((hosts, send_rows, width), BF16),
            pltpu.VMEM((2, n, local_count, slots, width), BF16),
            pltpu.VMEM((n * row_count, hidden), BF16),
            pltpu.VMEM((n * row_count, hidden), BF16),
            pltpu.VMEM((2, n, row_count, width), BF16),
            pltpu.VMEM((width, hidden), BF16),
            pltpu.VMEM((hidden, width), BF16),
            *(pltpu.VMEM(shape if reduce_here else (16, 128), BF16) for shape in reduce_shapes),
            pltpu.VMEM((local_count, width, units), BF16),
            pltpu.VMEM((local_count, units, width), BF16),
            pltpu.VMEM((local_count, all_rows, units), BF16),
            pltpu.VMEM((local_count, all_rows, units), BF16),
            pltpu.VMEM((2, local_count, n, slots, width), BF16),
            pltpu.VMEM((2, n - 1, row_count, width), BF16),
            pltpu.VMEM((2, local_count, n - 1, slots, width), BF16),
            pltpu.VMEM((2, hosts, back_rows, width), BF16),
            dma((1 + local_count, 2)),
            dma((local_count, 2)),
            dma((2, n - 1)),
            dma((2, n - 1)),
            dma((hosts - 1,)),
            dma((hosts - 1,)),
            dma((2, n - 1)),
            dma((2, n - 1)),
            dma((2, n - 1)),
            dma((2, n - 1)),
            dma((2, local_count, n - 1)),
            dma((2, local_count, n - 1)),
            dma((2, hosts - 1)),
            dma((2, hosts - 1)),
            dma((2 * chips,)),
            dma((2 * chips,)),
            dma((2, chips - 1)),
            dma((2, chips - 1)),
            dma((2,)),
            dma((2,)),
            dma((3,)),
        ],
        compiler_params=pltpu.CompilerParams(
            collective_id=0, has_side_effects=True, vmem_limit_bytes=64 * 2**20 - 2**17
        ),
        name="layer",
    )(
        tokens, cotangent, sendbuf, perm, gate_kept[:, None], kept_float[:, None], pick, unperm,
        residual_in, residual_out, expert_in, expert_out,
    )
    if not reduce_here:
        in_total, out_total = lax.psum((in_total, out_total), "expert")
    return (
        output,
        grad_tokens,
        grad_gate[:, 0],
        grad_expert_in,
        grad_expert_out,
        in_total,
        out_total,
    )


def solution(mesh):
    return jax.shard_map(
        on_device,
        mesh=mesh,
        in_specs=(
            P(("dp", "expert"), None),
            P(("dp", "expert")),
            P(("dp", "expert")),
            P(("dp", "expert")),
            P(("dp", "expert")),
            P(("dp", "expert"), None),
            P("expert", None, "dp"),
            P("expert", "dp", None),
            P(None, "dp"),
            P("dp", None),
        ),
        out_specs=(
            P(("dp", "expert"), None),
            P(("dp", "expert"), None),
            P(("dp", "expert")),
            P("expert", None, "dp"),
            P("expert", "dp", None),
            P(None, "dp"),
            P("dp", None),
        ),
        check_vma=False,
    )
```

```python
import functools

import jax
import jax.numpy as jnp
import numpy as np
from jax import lax
from jax.experimental import pallas as pl
from jax.experimental.pallas import tpu as pltpu
from jax.sharding import PartitionSpec as P

MESH = pl.DeviceIdType.MESH
F32 = jnp.float32
BF16 = jnp.bfloat16
GELU_C = float(np.sqrt(2.0 / np.pi))


def mm(left, right, left_dim=1, right_dim=0):
    return lax.dot_general(
        left, right, (((left_dim,), (right_dim,)), ((), ())), preferred_element_type=F32
    )


def gelu_parts(v):
    square = v * v
    t = jnp.tanh(GELU_C * (v + 0.044715 * (square * v)))
    half = 0.5 * (1.0 + t)
    slope = half + (0.5 * v) * (1.0 - t * t) * (GELU_C * (1.0 + (3 * 0.044715) * square))
    return v * half, slope


def tile_of(size, want):
    while size % want:
        want //= 2
    return want


def tiles(size, want, body):
    step = tile_of(size, want)

    def one(i, carry):
        body(pl.ds(pl.multiple_of(i * step, step), step))
        return carry

    lax.fori_loop(0, size // step, one, 0)


def greet(dp_count, host_count):
    dp, ex = lax.axis_index("dp"), lax.axis_index("expert")
    barrier = pltpu.get_barrier_semaphore()
    for k in range(1, dp_count):
        pl.semaphore_signal(
            barrier, inc=1, device_id=(lax.rem(dp + k, dp_count), ex), device_id_type=MESH
        )
    for k in range(1, host_count):
        pl.semaphore_signal(
            barrier, inc=1, device_id=(dp, lax.rem(ex + k, host_count)), device_id_type=MESH
        )
    pl.semaphore_wait(barrier, dp_count - 1 + host_count - 1)
    return dp, ex


def layer_kernel(
    n, hosts, local_count, reduce_here,
    tok, cot, sendbuf, perm, gate, kept, pick, unperm, rin_hbm, rout_hbm, win_hbm, wout_hbm,
    output, grad_tokens, grad_gate, gin, gout, gwin, gwout,
    rin, rout, rows, arrived, colv, dhid, dgpre, partial, pin, pout, in1, out1, in2, out2,
    win, wout, hid, gpre, part, drecv_buf, erecv_buf, back,
    wsem, gsem, asend, arecv, bsend, brecv, hsend, hrecv, dsend, drecv, esend, erecv,
    csend, crecv, psend, precv, qsend, qrecv, ssend, srecv, lsem,
):
    loads = [pltpu.make_async_copy(rin_hbm, rin, wsem.at[0, 0]),
             pltpu.make_async_copy(rout_hbm, rout, wsem.at[0, 1])]
    for j in range(local_count):
        loads.append(pltpu.make_async_copy(win_hbm.at[j], win.at[j], wsem.at[1 + j, 0]))
        loads.append(pltpu.make_async_copy(wout_hbm.at[j], wout.at[j], wsem.at[1 + j, 1]))
    for c in loads:
        c.start()
    dp, ex = greet(n, hosts)
    sends = []

    def remote(src, dst, send_sem, recv_sem, to):
        c = pltpu.make_async_remote_copy(
            src_ref=src, dst_ref=dst, send_sem=send_sem, recv_sem=recv_sem,
            device_id=to, device_id_type=MESH,
        )
        c.start()
        sends.append(c)
        return c

    square = n == 4
    beside = lax.div(dp, 2) * 2 + 1 - lax.rem(dp, 2) if square else None
    across = lax.rem(dp + 2, n) if square else None

    def spread(srcs, buf, ssem, rsem):
        if not square:
            return [
                [remote(srcs[a], buf.at[a, dp], ssem.at[a, k - 1], rsem.at[a, k - 1],
                        (lax.rem(dp + k, n), ex)) for k in range(1, n)]
                for a in range(2)
            ]
        return [
            [remote(srcs[a], buf.at[a, dp], ssem.at[a, k], rsem.at[a, k], (to, ex))
             for k, to in enumerate((beside, across))]
            for a in range(2)
        ]

    def relay(copies, buf, ssem, rsem):
        if not square:
            return [c for pair in copies for c in pair]
        copies[0][1].wait_recv()
        f0 = remote(buf.at[0, across], buf.at[0, across], ssem.at[0, 2], rsem.at[0, 2], (beside, ex))
        copies[1][0].wait_recv()
        f1 = remote(buf.at[1, beside], buf.at[1, beside], ssem.at[1, 2], rsem.at[1, 2], (across, ex))
        return [copies[0][0], copies[1][1], f0, f1]

    row_count, width = tok.shape
    tokens_all = n * row_count
    hidden = rin.shape[1]
    rows[0, dp] = tok[...]
    rows[1, dp] = cot[...]
    dense = spread((tok, cot), rows, asend, arecv)
    a2a = [
        remote(sendbuf.at[to], arrived.at[ex], bsend.at[k - 1], brecv.at[k - 1], (dp, to))
        for k, to in ((k, lax.rem(ex + k, hosts)) for k in range(1, hosts))
    ]
    keep = pltpu.make_async_copy(sendbuf.at[ex], arrived.at[ex], lsem.at[2])
    keep.start()
    rest = relay(dense, rows, asend, arecv)
    mark = len(sends)
    for c in a2a:
        c.wait_recv()
    keep.wait()
    hr = arrived.shape[0] * arrived.shape[1]
    slots = colv.shape[3]

    def place(cols):
        got = arrived[:, :, cols].reshape(hr, cols.size)
        put = mm(perm[...], got).astype(BF16)
        colv[:, dp, :, :, cols] = put.reshape(2, local_count, slots, cols.size)

    tiles(width, 512, place)
    column = spread((colv.at[0, dp], colv.at[1, dp]), colv, hsend, hrecv)
    loads[0].wait()
    loads[1].wait()
    for c in rest:
        c.wait_recv()

    def dense_units(f):
        x = rows[0].reshape(tokens_all, width)
        g = rows[1].reshape(tokens_all, width)
        value, slope = gelu_parts(mm(x, rin[:, f]))
        h = value.astype(BF16)
        dhid[:, f] = h
        p = (slope * mm(g, rout[f, :], 1, 1)).astype(BF16)
        dgpre[:, f] = p
        pout[f, :] = mm(h, g, 0, 0).astype(BF16)
        pin[:, f] = mm(x, p, 0, 0).astype(BF16)

    tiles(hidden, 256, dense_units)

    chips = hosts // 2
    chip, core = lax.div(ex, 2), lax.rem(ex, 2)
    other = 1 - core
    sibling = chip * 2 + other
    pairs = ((pin, in1, in2, rin, gin), (pout, out1, out2, rout, gout))

    def block_of(ref, c, q):
        size = ref.shape[0] // hosts
        return pl.ds(pl.multiple_of((c * chips + q) * size, 16), size)

    def half_of(ref, c):
        size = ref.shape[0] // 2
        return pl.ds(pl.multiple_of(c * size, 16), size)

    if reduce_here:
        first = [
            remote(p.at[half_of(p, other)], r1, psend.at[i], precv.at[i], (dp, sibling))
            for i, (p, r1, r2, s, o) in enumerate(pairs)
        ]

    def dense_back(d):
        o = mm(dhid[...], rout[:, d]).astype(BF16)
        partial[0, :, :, d] = o.reshape(n, row_count, d.size)
        o = mm(dgpre[...], rin[d, :], 1, 1).astype(BF16)
        partial[1, :, :, d] = o.reshape(n, row_count, d.size)

    tiles(width, 256, dense_back)
    second = []
    if reduce_here:
        for i, (p, r1, r2, s, o) in enumerate(pairs):
            first[i].wait_recv()
            size = p.shape[0] // hosts
            for q in range(chips):
                at = pl.ds(q * size, size)
                s[at, :] = (p[block_of(p, core, q), :].astype(F32) + r1[at, :].astype(F32)).astype(BF16)
            for k in range(1, chips):
                q = lax.rem(chip + k, chips)
                second.append(remote(
                    s.at[pl.ds(pl.multiple_of(q * size, 16), size)], r2.at[k - 1],
                    psend.at[2 + i * (chips - 1) + k - 1], precv.at[2 + i * (chips - 1) + k - 1],
                    (dp, q * 2 + core),
                ))
    else:
        saves = [pltpu.make_async_copy(pin, gin, lsem.at[0]), pltpu.make_async_copy(pout, gout, lsem.at[1])]
        for c in saves:
            c.start()
    rest = relay(column, colv, hsend, hrecv)
    dense_rs = [
        remote(partial.at[a, to], drecv_buf.at[a, k - 1], dsend.at[a, k - 1], drecv.at[a, k - 1], (to, ex))
        for a in range(2) for k, to in ((k, lax.rem(dp + k, n)) for k in range(1, n))
    ]
    for c in rest:
        c.wait_recv()

    all_rows = n * slots
    units = win.shape[2]
    scatter = [[], []]

    def push(a, j):
        for k in range(1, n):
            to = lax.rem(dp + k, n)
            scatter[a].append(remote(
                part.at[a, j, to], erecv_buf.at[a, j, k - 1],
                esend.at[a, j, k - 1], erecv.at[a, j, k - 1], (to, ex),
            ))

    for j in range(local_count):
        loads[2 + 2 * j].wait()
        loads[3 + 2 * j].wait()

        def forward(f):
            x = colv[0, :, j].reshape(all_rows, width)
            g = colv[1, :, j].reshape(all_rows, width)
            value, slope = gelu_parts(mm(x, win[j, :, f]))
            hid[j, :, f] = value.astype(BF16)
            gpre[j, :, f] = (slope * mm(g, wout[j, f, :], 1, 1)).astype(BF16)

        tiles(units, 256, forward)

        def project(d):
            o = mm(hid[j], wout[j, :, d]).astype(BF16)
            part[0, j, :, :, d] = o.reshape(n, slots, d.size)

        tiles(width, 256, project)
        push(0, j)

        def project_back(d):
            o = mm(gpre[j], win[j, d, :], 1, 1).astype(BF16)
            part[1, j, :, :, d] = o.reshape(n, slots, d.size)

        tiles(width, 256, project_back)
        push(1, j)

    third = []
    near = lax.div(chip, 2) * 2 + 1 - lax.rem(chip, 2)
    far = lax.rem(chip + 2, chips)
    if reduce_here:
        saves = []
        for c in second:
            c.wait_recv()
        for i, (p, r1, r2, s, o) in enumerate(pairs):
            size = p.shape[0] // hosts
            total = s[pl.ds(pl.multiple_of(chip * size, 16), size), :].astype(F32)
            for k in range(chips - 1):
                total = total + r2[k].astype(F32)
            done = s.at[pl.ds(chips * size, size)]
            done[...] = total.astype(BF16)
            c = pltpu.make_async_copy(done, o.at[block_of(o, core, chip)], lsem.at[i])
            c.start()
            saves.append(c)
            if chips == 4:
                partners = (near, far)
            else:
                partners = [lax.rem(chip + k, chips) for k in range(1, chips)]
            for k, q in enumerate(partners, 1):
                third.append(remote(
                    done, o.at[block_of(o, core, chip)],
                    qsend.at[i, k - 1], qrecv.at[i, k - 1], (dp, q * 2 + core),
                ))

    grads = []
    for j in range(local_count):

        def weights(f):
            g = colv[1, :, j].reshape(all_rows, width)
            wout[j, f, :] = mm(hid[j, :, f], g, 0, 0).astype(BF16)
            x = colv[0, :, j].reshape(all_rows, width)
            win[j, :, f] = mm(x, gpre[j, :, f], 0, 0).astype(BF16)

        tiles(units, 256, weights)
        for s, (src, dst) in enumerate(((win, gwin), (wout, gwout))):
            c = pltpu.make_async_copy(src.at[j], dst.at[j], gsem.at[j, s])
            c.start()
            grads.append(c)

    if reduce_here and chips == 4:
        for i, (p, r1, r2, s, o) in enumerate(pairs):
            third[2 * i + 1].wait_recv()
        third = [third[0], third[2]] + [
            remote(
                pair[4].at[block_of(pair[4], core, far)], pair[4].at[block_of(pair[4], core, far)],
                qsend.at[i, 2], qrecv.at[i, 2], (dp, near * 2 + core),
            )
            for i, pair in enumerate(pairs)
        ]

    back_rows = back.shape[2]
    back_all = hosts * back_rows
    back_copies = [[], []]
    per = row_count // back_rows

    def rows_for(a, host):
        start = pl.multiple_of(lax.rem(host, per) * back_rows, back_rows)
        return rows.at[a, lax.div(host, per), pl.ds(start, back_rows)]

    for c in sends[:mark]:
        c.wait_send()
    for a in range(2):
        for c in scatter[a]:
            c.wait_recv()

        def collect(d):
            total = part[a, :, dp, :, d].astype(F32)
            for k in range(n - 1):
                total = total + erecv_buf[a, :, k, :, d].astype(F32)
            summed = total.astype(BF16).reshape(local_count * slots, d.size)
            o = mm(unperm[...], summed).astype(BF16)
            rows[a, :hosts // per, :, d] = o.reshape(hosts // per, row_count, d.size)

        tiles(width, 256, collect)
        for k in range(1, hosts):
            to = lax.rem(ex + k, hosts)
            back_copies[a].append(remote(
                rows_for(a, to), back.at[a, ex], csend.at[a, k - 1], crecv.at[a, k - 1], (dp, to)
            ))
        back[a, ex] = rows_for(a, ex)[...]
    fourth = []
    if reduce_here:
        for c in saves:
            c.wait()
        for c in third:
            c.wait_recv()
        for i, (p, r1, r2, s, o) in enumerate(pairs):
            fourth.append(remote(
                o.at[half_of(o, core)], o.at[half_of(o, core)], ssend.at[i], srecv.at[i], (dp, sibling)
            ))
        saves = []
    for c in dense_rs:
        c.wait_recv()

    for a in range(2):
        for c in back_copies[a]:
            c.wait_recv()
        for lo in range(0, width, tile_of(width, 512)):
            d = pl.ds(lo, tile_of(width, 512))
            total = partial[a, dp, :, d].astype(F32)
            for k in range(n - 1):
                total = total + drecv_buf[a, k, :, d].astype(F32)
            mine = mm(pick[...], back[a, :, :, d].reshape(back_all, d.size))
            if a == 0:
                output[:, d] = (total + gate[...] * mine).astype(BF16)
                term = jnp.sum(cot[:, d].astype(F32) * mine, axis=1, keepdims=True)
                gg = term if lo == 0 else gg + term
            else:
                grad_tokens[:, d] = (total + mine).astype(BF16)
        if a == 0:
            grad_gate[...] = kept[...] * gg
    for c in grads + saves:
        c.wait()
    for c in fourth:
        c.wait_recv()
    for c in sends[mark:]:
        c.wait_send()


def ceil16(v):
    return -(-v // 16) * 16


def on_device(
    tokens, gate_prob, expert_index, slot_index, dropped, cotangent,
    expert_in, expert_out, residual_in, residual_out,
):
    n = lax.axis_size("dp")
    hosts = lax.axis_size("expert")
    local_count, width, units = expert_in.shape
    hidden = residual_in.shape[1]
    experts_all = local_count * hosts
    row_count = tokens.shape[0]
    capacity = max(2, 5 * row_count // (4 * experts_all))
    kept = (dropped == 0) & (slot_index < capacity)
    kept_float = kept.astype(F32)
    gate_kept = gate_prob * kept_float
    block = local_count * capacity
    send_rows = ceil16(2 * block)
    back_rows = ceil16(block)
    slots = ceil16(hosts * capacity)

    host = expert_index // local_count
    within = (expert_index % local_count) * capacity + slot_index
    send_pos = jnp.where(kept, host * send_rows + within, -1)
    back_pos = jnp.where(kept, host * back_rows + within, -1)
    scaled = (cotangent.astype(F32) * gate_kept[:, None]).astype(BF16)
    target = jnp.arange(hosts * send_rows, dtype=jnp.int32)[:, None]
    grad_pos = jnp.where(kept, send_pos + block, -1)
    place = jnp.concatenate(
        [(target == send_pos[None]).astype(BF16), (target == grad_pos[None]).astype(BF16)], axis=1
    )
    sendbuf = mm(place, jnp.concatenate([tokens, scaled], axis=0)).astype(BF16)
    sendbuf = sendbuf.reshape(hosts, send_rows, width)
    pick = (jnp.arange(hosts * back_rows, dtype=jnp.int32)[None] == back_pos[:, None]).astype(BF16)

    perm = np.zeros((2, local_count, slots, hosts, send_rows), np.float32)
    unperm = np.zeros((hosts, back_rows, local_count, slots), np.float32)
    for j in range(local_count):
        for h in range(hosts):
            for c in range(capacity):
                unperm[h, j * capacity + c, j, h * capacity + c] = 1
                for a in range(2):
                    perm[a, j, h * capacity + c, h, a * block + j * capacity + c] = 1
    perm = jnp.asarray(perm.reshape(2 * local_count * slots, hosts * send_rows), BF16)
    unperm = jnp.asarray(unperm.reshape(hosts * back_rows, local_count * slots), BF16)

    vmem = pl.BlockSpec(memory_space=pltpu.VMEM)
    anyspace = pl.BlockSpec(memory_space=pl.ANY)
    dma = pltpu.SemaphoreType.DMA
    all_rows = n * slots
    reduce_here = hosts % 2 == 0 and width % (16 * hosts) == 0 and hidden % (16 * hosts) == 0
    chips = hosts // 2
    reduce_shapes = (
        (width // 2, hidden),
        (hidden // 2, width),
        (chips - 1, width // hosts, hidden),
        (chips - 1, hidden // hosts, width),
    )
    output, grad_tokens, grad_gate, in_total, out_total, grad_expert_in, grad_expert_out = pl.pallas_call(
        functools.partial(layer_kernel, n, hosts, local_count, reduce_here),
        out_shape=(
            jax.ShapeDtypeStruct((row_count, width), BF16),
            jax.ShapeDtypeStruct((row_count, width), BF16),
            jax.ShapeDtypeStruct((row_count, 1), F32),
            jax.ShapeDtypeStruct((width, hidden), BF16),
            jax.ShapeDtypeStruct((hidden, width), BF16),
            jax.ShapeDtypeStruct((local_count, width, units), BF16),
            jax.ShapeDtypeStruct((local_count, units, width), BF16),
        ),
        in_specs=[vmem] * 2 + [anyspace] + [vmem] * 5 + [anyspace] * 4,
        out_specs=(vmem, vmem, vmem, anyspace, anyspace, anyspace, anyspace),
        scratch_shapes=[
            pltpu.VMEM((width, hidden), BF16),
            pltpu.VMEM((hidden, width), BF16),
            pltpu.VMEM((2, n, row_count, width), BF16),
            pltpu.VMEM((hosts, send_rows, width), BF16),
            pltpu.VMEM((2, n, local_count, slots, width), BF16),
            pltpu.VMEM((n * row_count, hidden), BF16),
            pltpu.VMEM((n * row_count, hidden), BF16),
            pltpu.VMEM((2, n, row_count, width), BF16),
            pltpu.VMEM((width, hidden), BF16),
            pltpu.VMEM((hidden, width), BF16),
            *(pltpu.VMEM(shape if reduce_here else (16, 128), BF16) for shape in reduce_shapes),
            pltpu.VMEM((local_count, width, units), BF16),
            pltpu.VMEM((local_count, units, width), BF16),
            pltpu.VMEM((local_count, all_rows, units), BF16),
            pltpu.VMEM((local_count, all_rows, units), BF16),
            pltpu.VMEM((2, local_count, n, slots, width), BF16),
            pltpu.VMEM((2, n - 1, row_count, width), BF16),
            pltpu.VMEM((2, local_count, n - 1, slots, width), BF16),
            pltpu.VMEM((2, hosts, back_rows, width), BF16),
            dma((1 + local_count, 2)),
            dma((local_count, 2)),
            dma((2, n - 1)),
            dma((2, n - 1)),
            dma((hosts - 1,)),
            dma((hosts - 1,)),
            dma((2, n - 1)),
            dma((2, n - 1)),
            dma((2, n - 1)),
            dma((2, n - 1)),
            dma((2, local_count, n - 1)),
            dma((2, local_count, n - 1)),
            dma((2, hosts - 1)),
            dma((2, hosts - 1)),
            dma((2 * chips,)),
            dma((2 * chips,)),
            dma((2, chips - 1)),
            dma((2, chips - 1)),
            dma((2,)),
            dma((2,)),
            dma((3,)),
        ],
        compiler_params=pltpu.CompilerParams(
            collective_id=0, has_side_effects=True, vmem_limit_bytes=64 * 2**20 - 2**17
        ),
        name="layer",
    )(
        tokens, cotangent, sendbuf, perm, gate_kept[:, None], kept_float[:, None], pick, unperm,
        residual_in, residual_out, expert_in, expert_out,
    )
    if not reduce_here:
        in_total, out_total = lax.psum((in_total, out_total), "expert")
    return (
        output,
        grad_tokens,
        grad_gate[:, 0],
        grad_expert_in,
        grad_expert_out,
        in_total,
        out_total,
    )


def solution(mesh):
    return jax.shard_map(
        on_device,
        mesh=mesh,
        in_specs=(
            P(("dp", "expert"), None),
            P(("dp", "expert")),
            P(("dp", "expert")),
            P(("dp", "expert")),
            P(("dp", "expert")),
            P(("dp", "expert"), None),
            P("expert", None, "dp"),
            P("expert", "dp", None),
            P(None, "dp"),
            P("dp", None),
        ),
        out_specs=(
            P(("dp", "expert"), None),
            P(("dp", "expert"), None),
            P(("dp", "expert")),
            P("expert", None, "dp"),
            P("expert", "dp", None),
            P(None, "dp"),
            P("dp", None),
        ),
        check_vma=False,
    )
```
